32 devices in a mesh: tm: 4 (over x, core), slope: 8 (over z, y).
Axes of the slice: x: 2, y: 2, z: 4, core: 2. Of those that a mesh axis runs over, the one named last changes fastest.
Arguments:
- telemetry: bfloat16 [8, 128, 96, 4096], P('slope', None, None, 'tm'), may hold values from -24 to 24
- frame_ids: int32 [4096], P('tm'), may hold values from 0 to 1023, as said below
- valid: int32 [8, 48], replicated, may hold values 0 or 1
- noise: float32 [1024], replicated, may hold values from 0.1 to 1
- prior_next: float32 [8, 128, 96, 1024], P('slope', 'tm'), may hold values from -2 to 2
Outputs:
- panel: float32 [8, 128, 96, 1024], P('slope', 'tm')
- next_block: float32 [8, 128, 96, 1024], P('slope', 'tm')
The draws below stay inside these ranges and needn't reach their ends.
Inputs may be any that keep to these rules, and one draw needn't show every extreme that they name: `frame_ids`: entry f names a frame of the block of 1024 buffer frames that starts at (f // 1024) * 1024; entries may repeat.
All inputs are finite; a program needn't handle non-finite values.
Results may differ from the reference program's by a relative error of at most 0.0003.
Values may be sent and summed in bfloat16 or wider, within the bound.
A program may use at most 256 MiB of HBM per device.

```python
import math
import jax
import jax.numpy as jnp
from jax import lax

M = 98304
B = 1024
SENSORS = 8
SEGS = 48
FR_DEV = 1024
FRAMES = 4096
RB = 128
CYC = 96
N_SLOPE = 8


def draw_telemetry(key, part):
    keys = jax.random.split(key, 3)
    full_shape = (N_SLOPE, RB, CYC, FRAMES)
    noise_part = jax.random.truncated_normal(keys[0], -4.0, 4.0, full_shape)
    strength = 0.6
    amplitudes = jax.random.truncated_normal(keys[1], -3.0, 3.0, (2, FRAMES))
    loadings = jax.random.truncated_normal(keys[2], -3.0, 3.0, (2, N_SLOPE, RB, CYC, 1))
    common = loadings[0] * amplitudes[0] + loadings[1] * amplitudes[1]
    return (noise_part + strength * common).astype(jnp.bfloat16)


def draw_frame_ids(key, part):
    picks = jax.random.randint(key, (FRAMES,), 0, FR_DEV, dtype=jnp.int32)
    picks = picks.at[0].set(FR_DEV - 1)
    return picks.at[FRAMES - 1].set(0)


def touch_ends(drawn, rng, low, largest):
    spot = [jax.random.randint(jax.random.fold_in(rng, axis), (), 0, length) for axis, length in enumerate(drawn.shape)]
    longest = drawn.shape.index(max(drawn.shape))
    neighbour = spot[:longest] + [(spot[longest] + 1) % drawn.shape[longest]] + spot[longest + 1:]
    return drawn.at[tuple(spot)].set(low).at[tuple(neighbour)].set(largest)


def levels(key, dims, shards, smallest, top_value):
    level = 1.0
    for position, blocks in shards:
        draws = jax.random.uniform(jax.random.fold_in(jax.random.fold_in(key, 6), position), (blocks,), jnp.float32, smallest / len(shards), top_value / len(shards))
        level = level * jnp.repeat(jnp.exp(draws), dims[position] // blocks).reshape((-1,) + (1,) * (len(dims) - 1 - position))
    return level


def gaussian(rng, extent, deviation, reach, pieces=(), kind=jnp.bfloat16):
    factor_of = levels(rng, extent, pieces, -0.22, 0.18) if pieces else 1.0
    entries = jax.random.normal(rng, extent, jnp.float32) * deviation * factor_of
    return jnp.minimum(jnp.maximum(entries, -reach), reach).astype(kind)


def setup_inputs(seed: int = 0) -> dict:
    splits = jax.random.split(jax.random.key(seed), 6)
    return {
        "telemetry": draw_telemetry(jax.random.fold_in(splits[5], 71), 0),
        "frame_ids": draw_frame_ids(jax.random.fold_in(splits[5], 71), 0),
        "valid": touch_ends((jax.random.randint(splits[2], (SENSORS, SEGS), 0, 4) < 3).astype(jnp.int32), jax.random.fold_in(splits[2], 1), 0, 1),
        "noise": jnp.clip(jnp.exp(jax.random.uniform(splits[3], (B,), jnp.float32, math.log(0.1), math.log(1.0))), 0.1, 1.0),
        "prior_next": gaussian(splits[4], (N_SLOPE, RB, CYC, B), 0.3, 2.0, ((0, 8), (1, 4)), jnp.float32),
    }


def reference(telemetry, frame_ids, valid, noise, prior_next):
    positions = jnp.arange(FRAMES, dtype=jnp.int32)
    columns = positions // FR_DEV * FR_DEV + frame_ids.astype(jnp.int32)
    slope_ids = (jnp.arange(CYC, dtype=jnp.int32)[None, None, :] * N_SLOPE + jnp.arange(N_SLOPE, dtype=jnp.int32)[:, None, None]) * RB + jnp.arange(RB, dtype=jnp.int32)[None, :, None]
    per_sensor = M // SENSORS
    seg_len = per_sensor // SEGS
    keep_row = valid[slope_ids // per_sensor, slope_ids % per_sensor // seg_len].astype(jnp.bfloat16)

    def select_cycle(cycle_id):
        tel_cycle = lax.dynamic_index_in_dim(telemetry, cycle_id, 2, keepdims=False)
        mask_cycle = lax.dynamic_index_in_dim(keep_row, cycle_id, 2, keepdims=False)
        return jnp.take(tel_cycle, columns, axis=2) * mask_cycle[:, :, None]
    first_cols = select_cycle(0).reshape(B, FRAMES)

    def gram_cycle(cycle_id):
        row_slice = select_cycle(cycle_id).reshape(B, FRAMES)
        return jnp.dot(row_slice.astype(jnp.float32), first_cols.T.astype(jnp.float32), preferred_element_type=jnp.float32)
    stacked = lax.map(gram_cycle, jnp.arange(CYC, dtype=jnp.int32)) / FRAMES
    stacked = stacked.at[0].add(jnp.diag(noise))
    factor = jnp.linalg.cholesky(stacked[0])
    inverse = jax.scipy.linalg.solve_triangular(factor, jnp.eye(B, dtype=factor.dtype), lower=True)
    flat_block = stacked.reshape(CYC * B, B)
    panel_flat = jnp.dot(flat_block, inverse.T, precision=lax.Precision.HIGHEST)
    second = panel_flat[B:2 * B]
    update = jnp.dot(panel_flat, second.T, precision=lax.Precision.HIGHEST)
    panel = panel_flat.reshape(CYC, N_SLOPE, RB, B).transpose(1, 2, 0, 3)
    next_block = prior_next - update.reshape(CYC, N_SLOPE, RB, B).transpose(1, 2, 0, 3)
    return (panel, next_block)
```

```python
import jax
import jax.numpy as jnp
from jax import lax
from jax.sharding import PartitionSpec as P


def dot_hi(a, b, dims):
    return lax.dot_general(
        a, b, (dims, ((), ())), precision=lax.Precision.HIGHEST, preferred_element_type=jnp.float32
    )


def block_inverse(diag_block, size):
    width = diag_block.shape[0]
    steps = width // size
    eye = jnp.eye(size, dtype=jnp.float32)
    trail = diag_block
    inv_rows = []
    low_cols = []
    for step in range(steps):
        pivot = trail[:size, :size]
        low = lax.linalg.cholesky(pivot, symmetrize_input=False)
        low_inv = lax.linalg.triangular_solve(low, eye, left_side=True, lower=True)
        base = step * size
        if step == 0:
            inv_row = low_inv
        else:
            left = jnp.concatenate(
                [c[base - (k + 1) * size : base - (k + 1) * size + size] for k, c in enumerate(low_cols)], axis=1
            )
            stacked = jnp.concatenate(inv_rows, axis=0)[:, :base]
            part = dot_hi(left, stacked, ((1,), (0,)))
            inv_row = jnp.concatenate([-dot_hi(low_inv, part, ((1,), (0,))), low_inv], axis=1)
        inv_rows.append(jnp.pad(inv_row, ((0, 0), (0, width - base - size))))
        if step + 1 < steps:
            col = dot_hi(trail[size:, :size], low_inv, ((1,), (1,)))
            low_cols.append(col)
            trail = trail[size:, size:] - dot_hi(col, col, ((1,), (1,)))
    return jnp.concatenate(inv_rows, axis=0)


def shards(telemetry, frame_ids, valid, noise, prior_next):
    slope_count = lax.axis_size("slope")
    tm_count = lax.axis_size("tm")
    slope_index = lax.axis_index("slope")
    tm_index = lax.axis_index("tm")
    row_block = telemetry.shape[1]
    cycles = telemetry.shape[2]
    frames_dev = telemetry.shape[3]
    block_width = noise.shape[0]
    quarter = row_block // tm_count
    frames_total = frame_ids.shape[0] * tm_count
    rows_iota = lax.broadcasted_iota(jnp.int32, (row_block, cycles), 0)
    cycle_iota = lax.broadcasted_iota(jnp.int32, (row_block, cycles), 1)
    slope_ids = (cycle_iota * slope_count + slope_index) * row_block + rows_iota
    sensors, segments = valid.shape
    per_sensor = cycles * block_width // sensors
    seg_len = per_sensor // segments
    seg_codes = slope_ids // per_sensor * segments + slope_ids % per_sensor // seg_len
    labels = jnp.arange(sensors * segments, dtype=jnp.int32)
    keep_row = jnp.sum(jnp.where(seg_codes[:, :, None] == labels, valid.reshape(-1), 0), axis=2).astype(jnp.float32)

    lead = telemetry[0, :, 0, :] * keep_row[:, 0:1].astype(jnp.bfloat16)
    first_raw = lax.all_gather(lead, "slope", axis=0, tiled=True)
    slots = lax.broadcasted_iota(jnp.int32, (frame_ids.shape[0], frames_dev), 1)
    counts = jnp.sum((frame_ids[:, None] == slots).astype(jnp.float32), axis=0)
    weighted = first_raw.astype(jnp.float32) * (counts / float(frames_total))[None, :]
    coarse = lax.reduce_precision(weighted, exponent_bits=8, mantissa_bits=7)
    high = coarse.astype(jnp.bfloat16)
    low = (weighted - coarse).astype(jnp.bfloat16)
    own = lax.dynamic_slice_in_dim(first_raw, slope_index * row_block, row_block, axis=0)

    def gram(rows, dims):
        return lax.dot_general(rows, high, (dims, ((), ())), preferred_element_type=jnp.float32) + lax.dot_general(
            rows, low, (dims, ((), ())), preferred_element_type=jnp.float32
        )

    full_cols = lax.broadcasted_iota(jnp.int32, (row_block, block_width), 1)
    own_ids = slope_index * row_block + lax.broadcasted_iota(jnp.int32, (row_block, block_width), 0)
    summed = lax.psum(gram(own, ((1,), (1,))), "tm")
    lead_rows = summed + jnp.where(full_cols == own_ids, noise[None, :], 0.0)
    diag_block = lax.all_gather(lead_rows, "slope", axis=0, tiled=True)

    partial = gram(telemetry[0], ((2,), (1,))) * keep_row[:, :, None]
    gram_block = lax.psum_scatter(partial, "tm", scatter_dimension=0, tiled=True)

    inverse = block_inverse(diag_block, 128)

    diag_cols = lax.broadcasted_iota(jnp.int32, (quarter, block_width), 1)
    diag_ids = (
        slope_index * row_block
        + tm_index * quarter
        + lax.broadcasted_iota(jnp.int32, (quarter, block_width), 0)
    )
    first_block = gram_block.at[:, 0, :].add(jnp.where(diag_cols == diag_ids, noise[None, :], 0.0))
    next_rows = dot_hi(first_block[:, 1, :], inverse, ((1,), (1,)))
    second = lax.all_gather(next_rows, ("slope", "tm"), axis=0, tiled=True)
    panel_rows = lax.dot_general(
        first_block, inverse, (((2,), (1,)), ((), ())),
        precision=lax.Precision.HIGHEST, preferred_element_type=jnp.float32,
    )
    update = lax.dot_general(
        panel_rows, second, (((2,), (1,)), ((), ())),
        precision=lax.Precision.HIGH, preferred_element_type=jnp.float32,
    )
    return (panel_rows[None], (prior_next[0] - update)[None])


def solution(mesh):
    return jax.shard_map(
        shards,
        mesh=mesh,
        in_specs=(P("slope", None, None, "tm"), P("tm"), P(), P(), P("slope", "tm", None, None)),
        out_specs=(P("slope", "tm", None, None), P("slope", "tm", None, None)),
        check_vma=False,
    )
```
